32 devices in a mesh: section: 2 (over x), expert: 16 (over z, y, core).
Axes of the slice: x: 2, y: 2, z: 4, core: 2. Of those that a mesh axis runs over, the one named last changes fastest.
Arguments:
- inputs: bfloat16 [2, 128, 2048], P(None, 'expert'), may hold values from -6 to 6
- route_ids: int32 [2, 2, 128, 8], P('section', None, 'expert'), may hold values from 0 to 15, all different within a row; in each aligned block of 8 rows (0 to 7, 8 to 15, ..., all dimensions but the last counted through in order) at most 8 rows name the same one
- route_gates: float32 [2, 2, 128, 8], P('section', None, 'expert'), may hold values from 0.1 to 1
- w_gate: bfloat16 [2, 16, 2048, 768], P('section', 'expert'), may hold values from -0.125 to 0.125
- w_up: bfloat16 [2, 16, 2048, 768], P('section', 'expert'), may hold values from -0.125 to 0.125
- w_down: bfloat16 [2, 16, 768, 2048], P('section', 'expert'), may hold values from -0.21875 to 0.21875
- cotangent: bfloat16 [2, 128, 2048], P(None, 'expert'), may hold values from -6 to 6
Outputs:
- section_out: bfloat16 [2, 2, 128, 2048], P('section', None, 'expert')
- grad_input: bfloat16 [2, 2, 128, 2048], P('section', None, 'expert')
- grad_gates: float32 [2, 2, 128, 8], P('section', None, 'expert')
- grad_w_gate: bfloat16 [2, 16, 2048, 768], P('section', 'expert')
- grad_w_up: bfloat16 [2, 16, 2048, 768], P('section', 'expert')
- grad_w_down: bfloat16 [2, 16, 768, 2048], P('section', 'expert')
The draws below stay inside these ranges and needn't reach their ends.
Inputs may be any that keep to these rules, and one draw needn't show every extreme that they name: `route_ids`: A token's 8 ids differ. In each layer and micro-batch, the 8 tokens of one device name no expert more than 8 times, a bound that some block reaches; every expert is named somewhere.
All inputs are finite; a program needn't handle non-finite values.
Results may differ from the reference program's by a relative error of at most 0.023.
Values may be sent and summed in bfloat16 or wider, within the bound.
A program may use at most 128 MiB of HBM per device.

```python
import math
import jax
import jax.numpy as jnp
import numpy as np
from jax import lax

D = 2048
FF = 768
TOP = 8
MB = 2
TOK_MB = 8
SECTIONS = 2
EXPERTS = 16
TOKENS = 128
MOST = 8
N_EXPERT = 16


def shard_levels(stream_key, dims, split, smallest, largest):
    def one(axis_at, blocks):
        draws = jax.random.uniform(jax.random.fold_in(jax.random.fold_in(stream_key, 6), axis_at), (blocks,), jnp.float32, smallest / len(split), largest / len(split))
        return jnp.repeat(jnp.exp(draws), dims[axis_at] // blocks).reshape((-1,) + (1,) * (len(dims) - axis_at - 1))

    gain = one(*split[0])
    for cut in split[1:]:
        gain = gain * one(*cut)
    return gain


def routed_block(own_key, own, number, rows, amount, top, most, slope):
    ranking = jax.random.permutation(own_key, amount)
    packed, usual = shares(amount, rows * top, most, slope, True), shares(amount, rows * top, most, slope, False)
    places = jnp.arange(amount)

    def named(tallies, offset_by):
        used = int((tallies > 0).sum())
        fixed = max(1, used // 4)
        moved = fixed + (places - fixed + offset_by * (used - fixed)) % max(1, amount - fixed)
        return jnp.zeros((amount,), jnp.int32).at[ranking[jnp.where(places < fixed, places, moved)]].set(jnp.asarray(tallies, jnp.int32))

    tallies = jnp.where(number % 4 == 0, named(packed, number // 4), named(usual, number - number // 4 - 1))
    mixed = jax.random.permutation(jax.random.fold_in(own, 3), amount)
    donor, sink = mixed[0:amount // 2 * 2:2], mixed[1:amount // 2 * 2:2]
    margin = jnp.minimum(tallies[donor] - 1, most - tallies[sink]) // 2
    margin = jnp.where((donor == ranking[0]) | (sink == ranking[0]) | (tallies[sink] == 0), 0, jnp.maximum(margin, 0))
    moved = jax.random.randint(jax.random.fold_in(own, 4), (amount // 2,), 0, 1 << 20) % (margin + 1)
    tallies = tallies.at[donor].add(-moved).at[sink].add(moved)
    items = jnp.searchsorted(jnp.cumsum(tallies), jnp.arange(rows * top), side="right").astype(jnp.int32)
    grid = items.reshape(top, rows).T
    grid = grid[jax.random.permutation(jax.random.fold_in(own, 1), rows)]
    offset_by = jax.random.randint(jax.random.fold_in(own, 2), (rows, 1), 0, top)
    return jnp.take_along_axis(grid, (jnp.arange(top)[None, :] + offset_by) % top, axis=1)


def shares(number_of, total, most, lean, full):
    weights = [(1 << 20) // math.isqrt(grade ** lean) + 1 for grade in range(1, number_of + 1)]
    largest = most if full else min(most, max(-(-total // number_of), total * weights[0] // sum(weights)))
    least = 1 if total - largest >= number_of - 1 else 0
    holding, surplus = [largest] + [least] * (number_of - 1), total - largest - least * (number_of - 1)
    while surplus > 0:
        candidates = [i for i in range(1, number_of) if holding[i] < largest] or [i for i in range(1, number_of) if holding[i] < most]
        whole, remaining = sum([weights[i] for i in candidates]), surplus
        for i in candidates:
            extra = min(most - holding[i], max(1, remaining * weights[i] // whole), surplus)
            holding[i] = holding[i] + extra
            surplus = surplus - extra
    return np.array(holding)


def scatter_about(stream_key, extent, width, bound, cuts=(), kind=jnp.bfloat16):
    drawn = jax.random.normal(stream_key, extent, jnp.float32) * width
    if len(cuts) > 0:
        drawn = shard_levels(stream_key, extent, cuts, -0.22, 0.18) * drawn
    return jnp.clip(drawn, min=-bound, max=bound).astype(kind)


def setup_inputs(seed: int = 0) -> dict:
    key_list = jax.random.split(jax.random.key(seed), 8)
    inputs = scatter_about(key_list[0], (MB, TOKENS, D), 1.0, 6.0, ((1, 16),))
    route_ids_keys = jax.random.split(jax.random.fold_in(key_list[1], 1), SECTIONS * MB * TOKENS // TOK_MB)
    route_ids_turns = jax.random.permutation(jax.random.fold_in(key_list[1], 3), SECTIONS * MB * TOKENS // TOK_MB)
    route_ids = jax.vmap(lambda own, number: routed_block(jax.random.fold_in(key_list[1], 2), own, number, TOK_MB, EXPERTS, TOP, MOST, 2))(route_ids_keys, route_ids_turns).reshape((SECTIONS, MB, TOKENS, TOP))
    route_gates = jnp.clip(jnp.exp(math.log(1.0) - 2.3025851 * jax.random.uniform(key_list[2], (SECTIONS, MB, TOKENS, TOP), jnp.float32) ** shard_levels(key_list[2], (SECTIONS, MB, TOKENS, TOP), ((0, 2), (2, 16)), -0.2, 0.2)), 0.1, 1.0)
    w_gate = scatter_about(key_list[3], (SECTIONS, EXPERTS, D, FF), D ** -0.5, 0.125, ((0, 2), (1, 16)))
    w_up = scatter_about(key_list[4], (SECTIONS, EXPERTS, D, FF), D ** -0.5, 0.125, ((0, 2), (1, 16)))
    w_down = scatter_about(key_list[5], (SECTIONS, EXPERTS, FF, D), FF ** -0.5, 0.21875, ((0, 2), (1, 16)))
    cotangent = scatter_about(key_list[6], (MB, TOKENS, D), 1.0, 6.0, ((1, 16),))
    return dict(inputs=inputs, route_ids=route_ids, route_gates=route_gates, w_gate=w_gate, w_up=w_up, w_down=w_down, cotangent=cotangent)


EPS = 1e-06

def route_slots(flat_ids, capacity):
    expert_ids = jnp.arange(EXPERTS, dtype=jnp.int32)
    onehot = (flat_ids[:, None] == expert_ids[None, :]).astype(jnp.int32)
    ranks = (jnp.cumsum(onehot, axis=0) - onehot).astype(jnp.int32)
    position = lax.optimization_barrier(jnp.sum(ranks * onehot, axis=1)).astype(jnp.int32)
    return (flat_ids * capacity + position).astype(jnp.int32)

def expert_forward(row_data, gate_mat, up_mat, down_mat):
    gate_pre = jnp.dot(row_data, gate_mat, preferred_element_type=jnp.float32)
    up_pre = jnp.dot(row_data, up_mat, preferred_element_type=jnp.float32)
    hidden = (gate_pre * jax.nn.sigmoid(gate_pre) * up_pre).astype(jnp.bfloat16)
    return jnp.dot(hidden, down_mat, preferred_element_type=jnp.float32).astype(jnp.bfloat16)

def expert_backward(row_data, grad_rows, gate_mat, up_mat, down_mat):
    gate_pre = jnp.dot(row_data, gate_mat, preferred_element_type=jnp.float32)
    up_pre = jnp.dot(row_data, up_mat, preferred_element_type=jnp.float32)
    sigma = jax.nn.sigmoid(gate_pre)
    active = gate_pre * sigma
    hidden = (active * up_pre).astype(jnp.bfloat16)
    grad_hidden = jnp.dot(grad_rows, down_mat.T, preferred_element_type=jnp.float32)
    grad_down = jnp.dot(hidden.T, grad_rows, preferred_element_type=jnp.float32)
    grad_gate_pre = (grad_hidden * up_pre * sigma * (1.0 + gate_pre * (1.0 - sigma))).astype(jnp.bfloat16)
    grad_up_pre = (grad_hidden * active).astype(jnp.bfloat16)
    grad_gate = jnp.dot(row_data.T, grad_gate_pre, preferred_element_type=jnp.float32)
    grad_up = jnp.dot(row_data.T, grad_up_pre, preferred_element_type=jnp.float32)
    grad_back = jnp.dot(grad_gate_pre, gate_mat.T, preferred_element_type=jnp.float32) + jnp.dot(grad_up_pre, up_mat.T, preferred_element_type=jnp.float32)
    return (grad_back.astype(jnp.bfloat16), grad_gate, grad_up, grad_down)

def layer_forward(layer_in, ids_now, gates_now, gate_all, up_all, down_all):
    capacity = N_EXPERT * MOST
    x_float = layer_in.astype(jnp.float32)
    scale = lax.rsqrt(lax.optimization_barrier(jnp.mean(x_float * x_float, axis=-1, keepdims=True)) + EPS)
    normed = (x_float * scale).astype(jnp.bfloat16)
    slot_index = route_slots(ids_now.reshape(-1).astype(jnp.int32), capacity)
    row_data = jnp.repeat(normed, TOP, axis=0)
    buffer = jnp.zeros((EXPERTS * capacity, D), jnp.bfloat16).at[slot_index].set(row_data)
    buffer = buffer.reshape(EXPERTS, capacity, D)
    results = lax.map(lambda items: expert_forward(items[0], items[1], items[2], items[3]), (buffer, gate_all, up_all, down_all))
    gathered = results.reshape(-1, D)[slot_index].reshape(TOKENS, TOP, D)
    mixed = x_float + lax.optimization_barrier(jnp.sum(gates_now[:, :, None] * gathered.astype(jnp.float32), axis=1))
    return (mixed.astype(jnp.bfloat16), buffer, gathered, slot_index, x_float, scale)

def layer_backward(layer_in, grad_out, ids_now, gates_now, gate_all, up_all, down_all):
    capacity = N_EXPERT * MOST
    mixed, buffer, gathered, slot_index, x_float, scale = layer_forward(layer_in, ids_now, gates_now, gate_all, up_all, down_all)
    grad_float = grad_out.astype(jnp.float32)
    grad_mix = lax.optimization_barrier(jnp.sum(grad_float[:, None, :] * gathered.astype(jnp.float32), axis=-1))
    grad_rows = (gates_now[:, :, None] * grad_float[:, None, :]).astype(jnp.bfloat16).reshape(-1, D)
    grad_buffer = jnp.zeros((EXPERTS * capacity, D), jnp.bfloat16).at[slot_index].set(grad_rows)
    grad_buffer = grad_buffer.reshape(EXPERTS, capacity, D)
    grad_back, grad_gate, grad_up, grad_down = lax.map(lambda items: expert_backward(items[0], items[1], items[2], items[3], items[4]), (buffer, grad_buffer, gate_all, up_all, down_all))
    grad_norm = lax.optimization_barrier(jnp.sum(grad_back.reshape(-1, D)[slot_index].reshape(TOKENS, TOP, D).astype(jnp.float32), axis=1))
    inner = lax.optimization_barrier(jnp.mean(grad_norm * x_float, axis=-1, keepdims=True))
    grad_in = grad_float + scale * grad_norm - x_float * (scale * scale * scale) * inner
    return (grad_in.astype(jnp.bfloat16), grad_mix, grad_gate, grad_up, grad_down)

def reference(inputs, route_ids, route_gates, w_gate, w_up, w_down, cotangent):
    layer_inputs = []
    layer_outputs = []
    for section_number in range(SECTIONS):
        ins_here = []
        outs_here = []
        for batch_number in range(MB):
            if section_number == 0:
                layer_in = inputs[batch_number]
            else:
                layer_in = layer_outputs[section_number - 1][batch_number]
            mixed = layer_forward(layer_in, route_ids[section_number, batch_number], route_gates[section_number, batch_number], w_gate[section_number], w_up[section_number], w_down[section_number])[0]
            ins_here.append(layer_in)
            outs_here.append(mixed)
        layer_inputs.append(ins_here)
        layer_outputs.append(outs_here)
    grad_inputs = [None] * SECTIONS
    grad_mixes = [None] * SECTIONS
    gate_grads = [None] * SECTIONS
    up_grads = [None] * SECTIONS
    down_grads = [None] * SECTIONS
    for section_number in reversed(range(SECTIONS)):
        ins_grad = []
        mix_grad = []
        gate_sum = jnp.zeros((EXPERTS, D, FF), jnp.float32)
        up_sum = jnp.zeros((EXPERTS, D, FF), jnp.float32)
        down_sum = jnp.zeros((EXPERTS, FF, D), jnp.float32)
        for batch_number in range(MB):
            if section_number == SECTIONS - 1:
                grad_out = cotangent[batch_number]
            else:
                grad_out = grad_inputs[section_number + 1][batch_number]
            grad_in, grad_mix, grad_gate, grad_up, grad_down = layer_backward(layer_inputs[section_number][batch_number], grad_out, route_ids[section_number, batch_number], route_gates[section_number, batch_number], w_gate[section_number], w_up[section_number], w_down[section_number])
            ins_grad.append(grad_in)
            mix_grad.append(grad_mix)
            gate_sum = gate_sum + grad_gate
            up_sum = up_sum + grad_up
            down_sum = down_sum + grad_down
        grad_inputs[section_number] = ins_grad
        grad_mixes[section_number] = mix_grad
        gate_grads[section_number] = gate_sum.astype(jnp.bfloat16)
        up_grads[section_number] = up_sum.astype(jnp.bfloat16)
        down_grads[section_number] = down_sum.astype(jnp.bfloat16)
    section_out = jnp.stack([jnp.stack(item) for item in layer_outputs])
    grad_input = jnp.stack([jnp.stack(item) for item in grad_inputs])
    grad_gates = jnp.stack([jnp.stack(item) for item in grad_mixes])
    return (section_out, grad_input, grad_gates, jnp.stack(gate_grads), jnp.stack(up_grads), jnp.stack(down_grads))
```

```python
import functools

import jax
import jax.numpy as jnp
from jax import lax
from jax.experimental import pallas as pl
from jax.experimental.pallas import tpu as pltpu
from jax.sharding import PartitionSpec as P

EPS = 1e-06
F32 = jnp.float32
BF16 = jnp.bfloat16
LANES = 128
TILE = 256


def nt_dot(a, b):
    return lax.dot_general(a, b, (((1,), (1,)), ((), ())), preferred_element_type=F32)


def bit_orders(n):
    bits = n.bit_length() - 1
    high_first = list(range(bits - 1, -1, -1))
    across = [1] + [b for b in high_first if b not in (0, 1)] + [0]
    return high_first, across


def kernel(
    sections, n, x_ref, ids_ref, gts_ref, cot_ref, wg_hbm, wu_hbm, wd_hbm,
    so_ref, gi_ref, gg_ref, nx_hbm, hg_hbm, ag_hbm, ggp_hbm, gup_hbm,
    wg, wu, wd, xin, gin, nown, xst, gst, agx, agg, tg, tt, ttr,
    gc, gp, up, hid, hg, ggp, gup, acc, sb, rb, sb0, rb0,
    ag_s, ag_r, rs_s, rs_r, rl_s, rl_r, loc,
):
    mb, tok, width = x_ref.shape
    top = ids_ref.shape[2]
    ff = wg.shape[1]
    steps = n.bit_length() - 1
    rows1 = n * tok
    rows = mb * rows1
    me = lax.axis_index("expert")
    sec = lax.axis_index("section")
    last = sections - 1
    orders = [bit_orders(n)[m % 2] for m in range(mb)]

    def bit_of(b):
        return (me // (1 << b)) % 2

    def peer(b):
        return me + (1 << b) * (1 - 2 * bit_of(b))

    place = [sum(bit_of(b) * (1 << k) for k, b in enumerate(order)) for order in orders]

    def other(m, k):
        r = place[m]
        return r + (1 << k) * (1 - 2 * ((r // (1 << k)) % 2))

    def base_of(r, k):
        return (r // (1 << k)) * (1 << k)

    def remote(src, dst, ssem, rsem, b):
        return pltpu.make_async_remote_copy(
            src_ref=src, dst_ref=dst, send_sem=ssem, recv_sem=rsem,
            device_id={"expert": peer(b)}, device_id_type=pl.DeviceIdType.MESH,
        )

    weights = [
        pltpu.make_async_copy(a, b, loc.at[i])
        for i, (a, b) in enumerate(((wg_hbm, wg), (wu_hbm, wu), (wd_hbm, wd)))
    ]
    for c in weights:
        c.start()

    barrier = pltpu.get_barrier_semaphore()
    for b in range(steps):
        pl.semaphore_signal(
            barrier, inc=1, device_id={"expert": peer(b)}, device_id_type=pl.DeviceIdType.MESH
        )

    def hello(ok, step):
        @pl.when(ok)
        def _():
            pl.semaphore_signal(
                barrier, inc=1, device_id={"section": sec + step},
                device_id_type=pl.DeviceIdType.MESH,
            )

    hello(sec > 0, -1)
    hello(sec < last, 1)

    lane = lax.broadcasted_iota(jnp.int32, (tok, LANES), 1)
    for m in range(mb):
        dense = jnp.zeros((tok, LANES), F32)
        for k in range(top):
            dense = dense + jnp.where(
                lane == ids_ref[m, :, k : k + 1], gts_ref[m, :, k : k + 1], 0.0
            )
        tg[m, place[m]] = dense

    beside = (sec > 0).astype(jnp.int32) + (sec < last).astype(jnp.int32)
    pl.semaphore_wait(barrier, steps + beside)

    def small_copy(m, k):
        part = tg.at[m, pl.ds(base_of(place[m], k), 1 << k)]
        return remote(part, part, ag_s.at[0, m, k], ag_r.at[0, m, k], orders[m][k])

    def row_copy(which, own, staged, full, m, k):
        sems = ag_s.at[which, m, k], ag_r.at[which, m, k]
        if k == 0:
            return remote(own.at[m], staged.at[m], *sems, orders[m][0])
        part = full.at[m, pl.ds(base_of(place[m], k) // 2, 1 << (k - 1))]
        return remote(part, part, *sems, orders[m][k])

    def gather_rows(which, own, staged, full):
        for k in range(steps):
            copies = [row_copy(which, own, staged, full, m, k) for m in range(mb)]
            for c in copies:
                c.start()
            for m, c in enumerate(copies):
                c.wait()
                if k == 0:
                    mine = own[m].astype(F32)
                    theirs = staged[m].astype(F32)
                    low = place[m] % 2 == 0
                    pair = jnp.concatenate(
                        [jnp.where(low, mine, theirs), jnp.where(low, theirs, mine)], axis=0
                    )
                    full[m, place[m] // 2] = pair.astype(BF16)

    def table_copy(m, k):
        theirs = base_of(other(m, k), k)
        return remote(
            tt.at[m, pl.ds(theirs, 1 << k)], ttr.at[m, pl.ds(1 << k, 1 << k)],
            rs_s.at[2, m, k], rs_r.at[2, m, k], orders[m][k],
        )

    def reduce_rows(which, table):
        def when_table(act):
            if table is True:
                act()
            elif table is not None:
                pl.when(table)(act)

        def row_part(m, k):
            sems = rs_s.at[which, m, k], rs_r.at[which, m, k]
            theirs = base_of(other(m, k), k)
            if k == 0:
                sb0[which, m] = acc[m, theirs].astype(BF16)
                return remote(sb0.at[which, m], rb0.at[which, m], *sems, orders[m][0])
            half = 1 << (k - 1)

            def pack(i, carry):
                pair = acc[m, pl.ds(theirs + 2 * i, 2)].reshape(2 * tok, width)
                sb[which, m, theirs // 2 + i] = pair.astype(BF16)
                return carry

            lax.fori_loop(0, half, pack, 0)
            return remote(
                sb.at[which, m, pl.ds(theirs // 2, half)], rb.at[which, m, pl.ds(half, half)],
                *sems, orders[m][k],
            )

        for k in reversed(range(steps)):
            copies = []
            for m in range(mb):
                copies.append(row_part(m, k))
                copies[m].start()

            def start_tables():
                for m in range(mb):
                    table_copy(m, k).start()

            when_table(start_tables)
            for m in range(mb):
                copies[m].wait()
                mine = base_of(place[m], k)
                if k == 0:
                    acc[m, mine] = acc[m, mine] + rb0[which, m].astype(F32)
                else:
                    half = 1 << (k - 1)

                    def add(i, carry):
                        got = rb[which, m, half + i].astype(F32).reshape(2, tok, width)
                        spot = pl.ds(mine + 2 * i, 2)
                        acc[m, spot] = acc[m, spot] + got
                        return carry

                    lax.fori_loop(0, half, add, 0)

            def finish_tables():
                for m in range(mb):
                    table_copy(m, k).wait()
                    mine = pl.ds(base_of(place[m], k), 1 << k)
                    tt[m, mine] = tt[m, mine] + ttr[m, pl.ds(1 << k, 1 << k)]

            when_table(finish_tables)

    @pl.when(sec == last)
    def _():
        gin[...] = cot_ref[...]
        gather_rows(2, gin, gst, agg)

    for k in range(steps):
        copies = [small_copy(m, k) for m in range(mb)]
        for c in copies:
            c.start()
        for c in copies:
            c.wait()
    all_lanes = lax.broadcasted_iota(jnp.int32, (rows, LANES), 1)
    gc[...] = jnp.sum(
        jnp.where(all_lanes == me, tg[...].reshape(rows, LANES), 0.0), axis=1, keepdims=True
    )

    def relay(which, src, dst, step):
        return pltpu.make_async_remote_copy(
            src_ref=src, dst_ref=dst, send_sem=rl_s.at[which], recv_sem=rl_r.at[which],
            device_id={"section": sec + step}, device_id_type=pl.DeviceIdType.MESH,
        )

    @pl.when(sec == 0)
    def _():
        xin[...] = x_ref[...]

    @pl.when(sec > 0)
    def _():
        relay(0, so_ref, xin, 0).wait_recv()

    x_float = xin[...].astype(F32)
    scale = lax.rsqrt(jnp.mean(x_float * x_float, axis=-1, keepdims=True) + EPS)
    nown[...] = (x_float * scale).astype(BF16)
    gather_rows(1, nown, xst, agx)
    keep = [pltpu.make_async_copy(agx, nx_hbm, loc.at[3])]
    keep[0].start()
    for c in weights:
        c.wait()

    def hidden_tile(j, carry):
        at = pl.ds(pl.multiple_of(j * TILE, TILE), TILE)
        data = agx[...].reshape(rows, width)
        gate = jnp.dot(data, wg[:, at], preferred_element_type=F32)
        upper = jnp.dot(data, wu[:, at], preferred_element_type=F32)
        gp[:, at] = gate
        up[:, at] = upper
        hid[:, at] = (gate * jax.nn.sigmoid(gate) * upper).astype(BF16)
        return carry

    lax.fori_loop(0, ff // TILE, hidden_tile, 0)

    def down_and_out(table):
        def down_tile(j, carry):
            at = pl.ds(pl.multiple_of(j * TILE, TILE), TILE)
            out = jnp.dot(hid[...], wd[:, at], preferred_element_type=F32) * gc[...]
            acc[:, :, :, at] = out.reshape(mb, n, tok, TILE)
            return carry

        lax.fori_loop(0, width // TILE, down_tile, 0)
        reduce_rows(0, table)
        for m in range(mb):
            so_ref[m] = (xin[m].astype(F32) + acc[m, place[m]]).astype(BF16)

    @pl.when(sec < last)
    def _():
        down_and_out(None)
        relay(0, so_ref, xin, 1).start()
        relay(1, gi_ref, gin, 0).wait_recv()
        gather_rows(2, gin, gst, agg)

    keep.append(pltpu.make_async_copy(agg, ag_hbm, loc.at[4]))
    keep[1].start()

    def back_tile(j, total):
        at = pl.ds(pl.multiple_of(j * TILE, TILE), TILE)
        raw = nt_dot(agg[...].reshape(rows, width), wd[at, :])
        gate, upper = gp[:, at], up[:, at]
        sigma = jax.nn.sigmoid(gate)
        active = gate * sigma
        total = total + jnp.sum(active * upper * raw, axis=1, keepdims=True)
        scaled = raw * gc[...]
        ggp[:, at] = (scaled * upper * sigma * (1.0 + gate * (1.0 - sigma))).astype(BF16)
        gup[:, at] = (scaled * active).astype(BF16)
        hg[:, at] = (active * upper * gc[...]).astype(BF16)
        return total

    total = lax.fori_loop(0, ff // TILE, back_tile, jnp.zeros((rows, 1), F32))
    tt[...] = jnp.where(all_lanes == me, total, 0.0).reshape(mb, n, tok, LANES)
    for i, (a, b) in enumerate(((hg, hg_hbm), (ggp, ggp_hbm), (gup, gup_hbm))):
        keep.append(pltpu.make_async_copy(a, b, loc.at[5 + i]))
        keep[-1].start()

    def norm_tile(j, carry):
        at = pl.ds(pl.multiple_of(j * TILE, TILE), TILE)
        out = nt_dot(ggp[...], wg[at, :]) + nt_dot(gup[...], wu[at, :])
        acc[:, :, :, at] = out.reshape(mb, n, tok, TILE)
        return carry

    lax.fori_loop(0, width // TILE, norm_tile, 0)
    reduce_rows(1, sec < last)
    for m in range(mb):
        xf = xin[m].astype(F32)
        sc = lax.rsqrt(jnp.mean(xf * xf, axis=-1, keepdims=True) + EPS)
        gn = acc[m, place[m]]
        inner = jnp.mean(gn * xf, axis=-1, keepdims=True)
        gi_ref[m] = (gin[m].astype(F32) + sc * gn - xf * (sc * sc * sc) * inner).astype(BF16)

    @pl.when(sec > 0)
    def _():
        relay(1, gi_ref, gin, -1).start()

    @pl.when(sec == last)
    def _():
        down_and_out(True)

    column = lax.broadcasted_iota(jnp.int32, (tok, top), 1)
    for m in range(mb):
        table = tt[m, place[m]]
        picked = jnp.zeros((tok, top), F32)
        for k in range(top):
            value = jnp.sum(
                jnp.where(lane == ids_ref[m, :, k : k + 1], table, 0.0), axis=1, keepdims=True
            )
            picked = picked + jnp.where(column == k, value, 0.0)
        gg_ref[m] = picked

    @pl.when(sec < last)
    def _():
        relay(0, so_ref, xin, 1).wait_send()

    @pl.when(sec > 0)
    def _():
        relay(1, gi_ref, gin, -1).wait_send()

    for c in keep:
        c.wait()


def body(sections, n, inputs, route_ids, route_gates, w_gate, w_up, w_down, cotangent):
    mb, tok, width = inputs.shape
    top = route_ids.shape[3]
    ff = w_gate.shape[3]
    rows = mb * n * tok
    steps = n.bit_length() - 1
    pairs = (mb, n // 2, 2 * tok, width)
    own = (mb, tok, width)
    vmem = pl.BlockSpec(memory_space=pltpu.VMEM)
    anywhere = pl.BlockSpec(memory_space=pl.ANY)
    sem = pltpu.SemaphoreType.DMA
    wide = pltpu.VMEM((rows, ff), BF16)
    table = pltpu.VMEM((mb, n, tok, LANES), F32)
    outs = pl.pallas_call(
        functools.partial(kernel, sections, n),
        out_shape=(
            jax.ShapeDtypeStruct(own, BF16),
            jax.ShapeDtypeStruct(own, BF16),
            jax.ShapeDtypeStruct((mb, tok, top), F32),
            jax.ShapeDtypeStruct(pairs, BF16),
            jax.ShapeDtypeStruct((rows, ff), BF16),
            jax.ShapeDtypeStruct(pairs, BF16),
            jax.ShapeDtypeStruct((rows, ff), BF16),
            jax.ShapeDtypeStruct((rows, ff), BF16),
        ),
        in_specs=[vmem] * 4 + [anywhere] * 3,
        out_specs=(vmem,) * 3 + (anywhere,) * 5,
        scratch_shapes=[
            pltpu.VMEM((width, ff), BF16),
            pltpu.VMEM((width, ff), BF16),
            pltpu.VMEM((ff, width), BF16),
            pltpu.VMEM(own, BF16),
            pltpu.VMEM(own, BF16),
            pltpu.VMEM(own, BF16),
            pltpu.VMEM(own, BF16),
            pltpu.VMEM(own, BF16),
            pltpu.VMEM(pairs, BF16),
            pltpu.VMEM(pairs, BF16),
            table,
            table,
            table,
            pltpu.VMEM((rows, 1), F32),
            pltpu.VMEM((rows, ff), F32),
            pltpu.VMEM((rows, ff), F32),
            wide,
            wide,
            wide,
            wide,
            pltpu.VMEM((mb, n, tok, width), F32),
            pltpu.VMEM((2,) + pairs, BF16),
            pltpu.VMEM((2,) + pairs, BF16),
            pltpu.VMEM((2,) + own, BF16),
            pltpu.VMEM((2,) + own, BF16),
            sem((3, mb, steps)),
            sem((3, mb, steps)),
            sem((3, mb, steps)),
            sem((3, mb, steps)),
            sem((2,)),
            sem((2,)),
            sem((8,)),
        ],
        compiler_params=pltpu.CompilerParams(
            collective_id=0, has_side_effects=True, vmem_limit_bytes=56 * 1024 * 1024
        ),
    )(
        inputs, route_ids[0], route_gates[0], cotangent, w_gate[0, 0], w_up[0, 0], w_down[0, 0]
    )
    section_out, grad_in, grad_gates, normed, scaled, grads, gate_pre, up_pre = outs
    normed = normed.reshape(rows, width)
    grads = grads.reshape(rows, width)

    def outer(a, b):
        return lax.dot_general(
            a, b, (((0,), (0,)), ((), ())), preferred_element_type=F32
        ).astype(BF16)[None, None]

    return (
        section_out[None],
        grad_in[None],
        grad_gates[None],
        outer(normed, gate_pre),
        outer(normed, up_pre),
        outer(scaled, grads),
    )


def solution(mesh):
    tokens = P(None, "expert", None)
    routed = P("section", None, "expert", None)
    held = P("section", "expert", None, None)
    return jax.shard_map(
        functools.partial(body, mesh.shape["section"], mesh.shape["expert"]),
        mesh=mesh,
        in_specs=(tokens, routed, routed, held, held, held, tokens),
        out_specs=(routed, routed, routed, held, held, held),
        check_vma=False,
    )
```

```python
import functools

import jax
import jax.numpy as jnp
from jax import lax
from jax.experimental import pallas as pl
from jax.experimental.pallas import tpu as pltpu
from jax.sharding import PartitionSpec as P

EPS = 1e-06
F32 = jnp.float32
BF16 = jnp.bfloat16
LANES = 128
TILE = 256
STAGED = 4


def nt_dot(a, b):
    return lax.dot_general(a, b, (((1,), (1,)), ((), ())), preferred_element_type=F32)


def bit_groups(n):
    bits = n.bit_length() - 1
    far = list(range(bits - 1, 1, -1))
    far = [tuple(far[i : i + 2]) for i in range(0, len(far), 2)]
    return far + [(1,), (0,)], [(1,)] + far + [(0,)]


def flip_mask(group, d):
    return sum(1 << b for i, b in enumerate(group) if (d >> i) & 1)


def kernel(
    sections, n, x_ref, ids_ref, gts_ref, cot_ref, wg_hbm, wu_hbm, wd_hbm,
    so_ref, gi_ref, gg_ref, nx_hbm, hg_hbm, ag_hbm, ggp_hbm, gup_hbm,
    wg, wu, wd, xin, gin, nown, xst, gst, agx, agg, tg, tt, ttr,
    gc, gp, up, hid, hg, ggp, gup, acc, sb, rb, sb0, rb0,
    ag_s, ag_r, rs_s, rs_r, rl_s, rl_r, loc,
):
    mb, tok, width = x_ref.shape
    top = ids_ref.shape[2]
    ff = wg.shape[1]
    steps = n.bit_length() - 1
    rows1 = n * tok
    rows = mb * rows1
    me = lax.axis_index("expert")
    sec = lax.axis_index("section")
    last = sections - 1
    groups = [bit_groups(n)[m % 2] for m in range(mb)]

    def bit_of(b):
        return (me // (1 << b)) % 2

    def flipped(mask):
        return me + sum(
            (1 << b) * (1 - 2 * bit_of(b)) for b in range(steps) if (mask >> b) & 1
        )

    stages, place = [], []
    for group in groups:
        listed, at, r = [], 0, 0
        for bits in group:
            listed.append((at, bits))
            r = r + sum(bit_of(b) * (1 << (at + i)) for i, b in enumerate(bits))
            at += len(bits)
        stages.append(listed)
        place.append(r)
    depth = len(stages[0])

    def other(m, low, d):
        r = place[m]
        for i in range(steps):
            if ((d << low) >> i) & 1:
                r = r + (1 << i) * (1 - 2 * ((place[m] // (1 << i)) % 2))
        return r

    def diffs(m, s):
        return range(1, 1 << len(stages[m][s][1]))

    def base_of(r, low):
        return (r // (1 << low)) * (1 << low)

    def remote(src, dst, ssem, rsem, mask):
        return pltpu.make_async_remote_copy(
            src_ref=src, dst_ref=dst, send_sem=ssem, recv_sem=rsem,
            device_id={"expert": flipped(mask)}, device_id_type=pl.DeviceIdType.MESH,
        )

    weights = [
        pltpu.make_async_copy(a, b, loc.at[i])
        for i, (a, b) in enumerate(((wg_hbm, wg), (wu_hbm, wu), (wd_hbm, wd)))
    ]
    for c in weights:
        c.start()

    barrier = pltpu.get_barrier_semaphore()
    masks = sorted(
        {flip_mask(bits, d) for group in groups for bits in group for d in range(1, 1 << len(bits))}
    )
    for mask in masks:
        pl.semaphore_signal(
            barrier, inc=1, device_id={"expert": flipped(mask)},
            device_id_type=pl.DeviceIdType.MESH,
        )

    def hello(ok, step):
        @pl.when(ok)
        def _():
            pl.semaphore_signal(
                barrier, inc=1, device_id={"section": sec + step},
                device_id_type=pl.DeviceIdType.MESH,
            )

    hello(sec > 0, -1)
    hello(sec < last, 1)

    lane = lax.broadcasted_iota(jnp.int32, (tok, LANES), 1)
    for m in range(mb):
        dense = jnp.zeros((tok, LANES), F32)
        for k in range(top):
            dense = dense + jnp.where(
                lane == ids_ref[m, :, k : k + 1], gts_ref[m, :, k : k + 1], 0.0
            )
        tg[m, place[m]] = dense

    beside = (sec > 0).astype(jnp.int32) + (sec < last).astype(jnp.int32)
    pl.semaphore_wait(barrier, len(masks) + beside)

    def small_copy(m, s, d):
        low, bits = stages[m][s]
        part = tg.at[m, pl.ds(base_of(place[m], low), 1 << low)]
        return remote(
            part, part, ag_s.at[0, m, d << low], ag_r.at[0, m, d << low], flip_mask(bits, d)
        )

    def row_copy(which, own, staged, full, m, s, d):
        low, bits = stages[m][s]
        sems = ag_s.at[which, m, d << low], ag_r.at[which, m, d << low]
        if low == 0:
            return remote(own.at[m], staged.at[m, d], *sems, flip_mask(bits, d))
        part = full.at[m, pl.ds(base_of(place[m], low) // 2, 1 << (low - 1))]
        return remote(part, part, *sems, flip_mask(bits, d))

    def every(build, act):
        for s in range(depth):
            for m in range(mb):
                for d in diffs(m, s):
                    act(build(m, s, d))

    def gather_rows(rows_of, small):
        for s in range(depth):
            for m in range(mb):
                for d in diffs(m, s):
                    if rows_of is not None:
                        row_copy(*rows_of, m, s, d).start()
                    if small:
                        small_copy(m, s, d).start()
            for m in range(mb):
                for d in diffs(m, s):
                    if rows_of is not None:
                        row_copy(*rows_of, m, s, d).wait_recv()
                    if small:
                        small_copy(m, s, d).wait_recv()
                if s == 0 and rows_of is not None:
                    _, own, staged, full = rows_of
                    even = place[m] % 2 == 0
                    for p in range(1 << (len(stages[m][0][1]) - 1)):
                        near = own[m] if p == 0 else staged[m, 2 * p]
                        near, off = near.astype(F32), staged[m, 2 * p + 1].astype(F32)
                        pair = jnp.concatenate(
                            [jnp.where(even, near, off), jnp.where(even, off, near)], axis=0
                        )
                        full[m, other(m, 0, 2 * p) // 2] = pair.astype(BF16)

    def table_copy(m, s, d):
        low, bits = stages[m][s]
        theirs = base_of(other(m, low, d), low)
        return remote(
            tt.at[m, pl.ds(theirs, 1 << low)], ttr.at[m, pl.ds(d << low, 1 << low)],
            rs_s.at[2, m, d << low], rs_r.at[2, m, d << low], flip_mask(bits, d),
        )

    def sum_copy(which, m, s, d):
        low, bits = stages[m][s]
        sems = rs_s.at[which, m, d << low], rs_r.at[which, m, d << low]
        if low == 0:
            return remote(sb0.at[which, m, d], rb0.at[which, m, d], *sems, flip_mask(bits, d))
        half = 1 << (low - 1)
        theirs = base_of(other(m, low, d), low)
        return remote(
            sb.at[which, m, pl.ds(theirs // 2, half)], rb.at[which, m, pl.ds(d * half, half)],
            *sems, flip_mask(bits, d),
        )

    def reduce_rows(which, table):
        def when_table(act):
            if table is True:
                act()
            elif table is not None:
                pl.when(table)(act)

        def pack(m, low, d):
            theirs = base_of(other(m, low, d), low)
            if low == 0:
                sb0[which, m, d] = acc[m, theirs].astype(BF16)
                return

            def one(i, carry):
                pair = acc[m, pl.ds(theirs + 2 * i, 2)].reshape(2 * tok, width)
                sb[which, m, theirs // 2 + i] = pair.astype(BF16)
                return carry

            lax.fori_loop(0, 1 << (low - 1), one, 0)

        for s in reversed(range(depth)):
            for m in range(mb):
                for d in diffs(m, s):
                    pack(m, stages[m][s][0], d)
                    sum_copy(which, m, s, d).start()

            def start_tables():
                for m in range(mb):
                    for d in diffs(m, s):
                        table_copy(m, s, d).start()

            when_table(start_tables)
            for m in range(mb):
                low = stages[m][s][0]
                mine = base_of(place[m], low)
                for d in diffs(m, s):
                    sum_copy(which, m, s, d).wait_recv()
                if low == 0:
                    whole = acc[m, mine]
                    for d in diffs(m, s):
                        whole = whole + rb0[which, m, d].astype(F32)
                    acc[m, mine] = whole
                else:
                    half = 1 << (low - 1)

                    def add(i, carry):
                        spot = pl.ds(mine + 2 * i, 2)
                        whole = acc[m, spot]
                        for d in diffs(m, s):
                            got = rb[which, m, d * half + i].astype(F32)
                            whole = whole + got.reshape(2, tok, width)
                        acc[m, spot] = whole
                        return carry

                    lax.fori_loop(0, half, add, 0)

            def finish_tables():
                for m in range(mb):
                    low = stages[m][s][0]
                    mine = pl.ds(base_of(place[m], low), 1 << low)
                    for d in diffs(m, s):
                        table_copy(m, s, d).wait_recv()
                        tt[m, mine] = tt[m, mine] + ttr[m, pl.ds(d << low, 1 << low)]

            when_table(finish_tables)

    x_rows = (1, nown, xst, agx)
    g_rows = (2, gin, gst, agg)

    def normalize():
        x_float = xin[...].astype(F32)
        scale = lax.rsqrt(jnp.mean(x_float * x_float, axis=-1, keepdims=True) + EPS)
        nown[...] = (x_float * scale).astype(BF16)

    def relay(which, src, dst, step):
        return pltpu.make_async_remote_copy(
            src_ref=src, dst_ref=dst, send_sem=rl_s.at[which], recv_sem=rl_r.at[which],
            device_id={"section": sec + step}, device_id_type=pl.DeviceIdType.MESH,
        )

    @pl.when(sec == last)
    def _():
        gin[...] = cot_ref[...]
        gather_rows(g_rows, True)

    @pl.when(sec == 0)
    def _():
        xin[...] = x_ref[...]
        normalize()
        gather_rows(x_rows, last > 0)

    @pl.when((sec > 0) & (sec < last))
    def _():
        gather_rows(None, True)

    @pl.when(sec > 0)
    def _():
        relay(0, so_ref, xin, 0).wait_recv()
        normalize()
        gather_rows(x_rows, False)

    all_lanes = lax.broadcasted_iota(jnp.int32, (rows, LANES), 1)
    gc[...] = jnp.sum(
        jnp.where(all_lanes == me, tg[...].reshape(rows, LANES), 0.0), axis=1, keepdims=True
    )

    keep = [pltpu.make_async_copy(agx, nx_hbm, loc.at[3])]
    keep[0].start()
    for c in weights:
        c.wait()

    def hidden_tile(j, carry):
        at = pl.ds(pl.multiple_of(j * TILE, TILE), TILE)
        data = agx[...].reshape(rows, width)
        gate = jnp.dot(data, wg[:, at], preferred_element_type=F32)
        upper = jnp.dot(data, wu[:, at], preferred_element_type=F32)
        gp[:, at] = gate
        up[:, at] = upper
        hid[:, at] = (gate * jax.nn.sigmoid(gate) * upper).astype(BF16)
        return carry

    lax.fori_loop(0, ff // TILE, hidden_tile, 0)

    def down_and_out(table):
        def down_tile(j, carry):
            at = pl.ds(pl.multiple_of(j * TILE, TILE), TILE)
            out = jnp.dot(hid[...], wd[:, at], preferred_element_type=F32) * gc[...]
            acc[:, :, :, at] = out.reshape(mb, n, tok, TILE)
            return carry

        lax.fori_loop(0, width // TILE, down_tile, 0)
        reduce_rows(0, table)
        for m in range(mb):
            so_ref[m] = (xin[m].astype(F32) + acc[m, place[m]]).astype(BF16)

    @pl.when(sec < last)
    def _():
        down_and_out(None)
        relay(0, so_ref, xin, 1).start()
        relay(1, gi_ref, gin, 0).wait_recv()
        gather_rows(g_rows, False)

    keep.append(pltpu.make_async_copy(agg, ag_hbm, loc.at[4]))
    keep[1].start()

    def back_tile(j, total):
        at = pl.ds(pl.multiple_of(j * TILE, TILE), TILE)
        raw = nt_dot(agg[...].reshape(rows, width), wd[at, :])
        gate, upper = gp[:, at], up[:, at]
        sigma = jax.nn.sigmoid(gate)
        active = gate * sigma
        total = total + jnp.sum(active * upper * raw, axis=1, keepdims=True)
        scaled = raw * gc[...]
        ggp[:, at] = (scaled * upper * sigma * (1.0 + gate * (1.0 - sigma))).astype(BF16)
        gup[:, at] = (scaled * active).astype(BF16)
        hg[:, at] = (active * upper * gc[...]).astype(BF16)
        return total

    total = lax.fori_loop(0, ff // TILE, back_tile, jnp.zeros((rows, 1), F32))
    tt[...] = jnp.where(all_lanes == me, total, 0.0).reshape(mb, n, tok, LANES)
    for i, (a, b) in enumerate(((hg, hg_hbm), (ggp, ggp_hbm), (gup, gup_hbm))):
        keep.append(pltpu.make_async_copy(a, b, loc.at[5 + i]))
        keep[-1].start()

    def norm_tile(j, carry):
        at = pl.ds(pl.multiple_of(j * TILE, TILE), TILE)
        out = nt_dot(ggp[...], wg[at, :]) + nt_dot(gup[...], wu[at, :])
        acc[:, :, :, at] = out.reshape(mb, n, tok, TILE)
        return carry

    lax.fori_loop(0, width // TILE, norm_tile, 0)
    reduce_rows(1, sec < last)
    for m in range(mb):
        xf = xin[m].astype(F32)
        sc = lax.rsqrt(jnp.mean(xf * xf, axis=-1, keepdims=True) + EPS)
        gn = acc[m, place[m]]
        inner = jnp.mean(gn * xf, axis=-1, keepdims=True)
        gi_ref[m] = (gin[m].astype(F32) + sc * gn - xf * (sc * sc * sc) * inner).astype(BF16)

    @pl.when(sec > 0)
    def _():
        relay(1, gi_ref, gin, -1).start()

    @pl.when(sec == last)
    def _():
        down_and_out(True)

    column = lax.broadcasted_iota(jnp.int32, (tok, top), 1)
    for m in range(mb):
        table = tt[m, place[m]]
        picked = jnp.zeros((tok, top), F32)
        for k in range(top):
            value = jnp.sum(
                jnp.where(lane == ids_ref[m, :, k : k + 1], table, 0.0), axis=1, keepdims=True
            )
            picked = picked + jnp.where(column == k, value, 0.0)
        gg_ref[m] = picked

    @pl.when(sec < last)
    def _():
        relay(0, so_ref, xin, 1).wait_send()

    @pl.when(sec > 0)
    def _():
        relay(1, gi_ref, gin, -1).wait_send()

    every(small_copy, lambda c: c.wait_send())
    every(table_copy, lambda c: c.wait_send())
    for rows_of in (x_rows, g_rows):
        every(functools.partial(row_copy, *rows_of), lambda c: c.wait_send())
    for which in range(2):
        every(functools.partial(sum_copy, which), lambda c: c.wait_send())
    for c in keep:
        c.wait()


def body(sections, n, inputs, route_ids, route_gates, w_gate, w_up, w_down, cotangent):
    mb, tok, width = inputs.shape
    top = route_ids.shape[3]
    ff = w_gate.shape[3]
    rows = mb * n * tok
    pairs = (mb, n // 2, 2 * tok, width)
    own = (mb, tok, width)
    staged = (mb, STAGED, tok, width)
    vmem = pl.BlockSpec(memory_space=pltpu.VMEM)
    anywhere = pl.BlockSpec(memory_space=pl.ANY)
    sem = pltpu.SemaphoreType.DMA
    wide = pltpu.VMEM((rows, ff), BF16)
    table = pltpu.VMEM((mb, n, tok, LANES), F32)
    outs = pl.pallas_call(
        functools.partial(kernel, sections, n),
        out_shape=(
            jax.ShapeDtypeStruct(own, BF16),
            jax.ShapeDtypeStruct(own, BF16),
            jax.ShapeDtypeStruct((mb, tok, top), F32),
            jax.ShapeDtypeStruct(pairs, BF16),
            jax.ShapeDtypeStruct((rows, ff), BF16),
            jax.ShapeDtypeStruct(pairs, BF16),
            jax.ShapeDtypeStruct((rows, ff), BF16),
            jax.ShapeDtypeStruct((rows, ff), BF16),
        ),
        in_specs=[vmem] * 4 + [anywhere] * 3,
        out_specs=(vmem,) * 3 + (anywhere,) * 5,
        scratch_shapes=[
            pltpu.VMEM((width, ff), BF16),
            pltpu.VMEM((width, ff), BF16),
            pltpu.VMEM((ff, width), BF16),
            pltpu.VMEM(own, BF16),
            pltpu.VMEM(own, BF16),
            pltpu.VMEM(own, BF16),
            pltpu.VMEM(staged, BF16),
            pltpu.VMEM(staged, BF16),
            pltpu.VMEM(pairs, BF16),
            pltpu.VMEM(pairs, BF16),
            table,
            table,
            table,
            pltpu.VMEM((rows, 1), F32),
            pltpu.VMEM((rows, ff), F32),
            pltpu.VMEM((rows, ff), F32),
            wide,
            wide,
            wide,
            wide,
            pltpu.VMEM((mb, n, tok, width), F32),
            pltpu.VMEM((2,) + pairs, BF16),
            pltpu.VMEM((2,) + pairs, BF16),
            pltpu.VMEM((2,) + staged, BF16),
            pltpu.VMEM((2,) + staged, BF16),
            sem((3, mb, n)),
            sem((3, mb, n)),
            sem((3, mb, n)),
            sem((3, mb, n)),
            sem((2,)),
            sem((2,)),
            sem((8,)),
        ],
        compiler_params=pltpu.CompilerParams(
            collective_id=0, has_side_effects=True, vmem_limit_bytes=56 * 1024 * 1024
        ),
    )(
        inputs, route_ids[0], route_gates[0], cotangent, w_gate[0, 0], w_up[0, 0], w_down[0, 0]
    )
    section_out, grad_in, grad_gates, normed, scaled, grads, gate_pre, up_pre = outs
    normed = normed.reshape(rows, width)
    grads = grads.reshape(rows, width)

    def outer(a, b):
        return lax.dot_general(
            a, b, (((0,), (0,)), ((), ())), preferred_element_type=F32
        ).astype(BF16)[None, None]

    return (
        section_out[None],
        grad_in[None],
        grad_gates[None],
        outer(normed, gate_pre),
        outer(normed, up_pre),
        outer(scaled, grads),
    )


def solution(mesh):
    tokens = P(None, "expert", None)
    routed = P("section", None, "expert", None)
    held = P("section", "expert", None, None)
    return jax.shard_map(
        functools.partial(body, mesh.shape["section"], mesh.shape["expert"]),
        mesh=mesh,
        in_specs=(tokens, routed, routed, held, held, held, tokens),
        out_specs=(routed, routed, routed, held, held, held),
        check_vma=False,
    )
```
